32 devices in a mesh: expert: 4 (over z), replica: 4 (over y, x), tensor: 2 (over core).
Axes of the slice: x: 2, y: 2, z: 4, core: 2. Of those that a mesh axis runs over, the one named last changes fastest.
Arguments:
- tokens: bfloat16 [2048, 2048], P(('expert', 'replica')), may hold values from -6 to 6
- cotangent: bfloat16 [2048, 2048], P(('expert', 'replica')), may hold values from -6 to 6
- routes: int32 [2048, 8], P(('expert', 'replica')), may hold values from 0 to 15, all different within a row; in each aligned block of 128 rows (0 to 127, 128 to 255, ...) at most 128 rows name the same one
- gates: float32 [2048, 8], P(('expert', 'replica')), may hold values from 0.05 to 1
- gate_weight: bfloat16 [16, 2048, 768], P('expert', None, 'tensor'), may hold values from -0.125 to 0.125
- up_weight: bfloat16 [16, 2048, 768], P('expert', None, 'tensor'), may hold values from -0.125 to 0.125
- down_weight: bfloat16 [16, 768, 2048], P('expert', 'tensor'), may hold values from -0.21875 to 0.21875
Outputs:
- token_grad: bfloat16 [2048, 2048], P(('expert', 'replica'), 'tensor')
- gate_weight_grad: bfloat16 [16, 2048, 768], P(('expert', 'replica'), None, 'tensor')
- up_weight_grad: bfloat16 [16, 2048, 768], P(('expert', 'replica'), None, 'tensor')
- down_weight_grad: bfloat16 [16, 768, 2048], P(('expert', 'replica'), 'tensor')
The draws below stay inside these ranges and needn't reach their ends.
Inputs may be any that keep to these rules, and one draw needn't show every extreme that they name: `routes`: each row names 8 different experts. Within each aligned block of 128 rows (the rows of one device) no expert is named by more than 128 rows, a bound that some block reaches.
All inputs are finite; a program needn't handle non-finite values.
Results may differ from the reference program's by a relative error of at most 0.0095.
Values may be sent and summed in bfloat16 or wider, within the bound.
No kernel may reach another device: no remote copies, remote signals or barrier semaphores. Data moves between devices by JAX's collectives and lax.ppermute only.
A program may use at most 192 MiB of HBM per device.

```python
import math
import jax
import jax.numpy as jnp
import numpy as np
from jax import lax

D = 2048
FF = 768
TOPK = 8
TOK_DEV = 128
EXPERTS = 16
TOKENS = 2048
CAP = 128
N_EXPERT = 4
N_REPLICA = 4
N_TENSOR = 2


def level_of(rng, extent, shards, low, top_value):
    level, own = 1.0, jax.random.fold_in(rng, 6)
    for dim, blocks in shards:
        steps = jnp.exp(jax.random.uniform(jax.random.fold_in(own, dim), (blocks,), jnp.float32, low / len(shards), top_value / len(shards)))
        level = level * jnp.repeat(steps, extent[dim] // blocks).reshape([-1 if axis == dim else 1 for axis in range(len(extent))])
    return level


def deal_out(rng, own, number, rows, count, top, reach, lean):
    order = jax.random.permutation(rng, count)
    crowded, ordinary = shares(count, rows * top, reach, lean, True), shares(count, rows * top, reach, lean, False)
    places = jnp.arange(count)

    def named(sizes, rotation):
        used = int((sizes > 0).sum())
        fixed = max(1, used // 4)
        passed = fixed + (places - fixed + rotation * (used - fixed)) % max(1, count - fixed)
        return jnp.zeros((count,), jnp.int32).at[order[jnp.where(places < fixed, places, passed)]].set(jnp.asarray(sizes, jnp.int32))

    sizes = jnp.where(number % 4 == 0, named(crowded, number // 4), named(ordinary, number - number // 4 - 1))
    mixed = jax.random.permutation(jax.random.fold_in(own, 3), count)
    donor, receiver = mixed[0:count // 2 * 2:2], mixed[1:count // 2 * 2:2]
    margin = jnp.minimum(sizes[donor] - 1, reach - sizes[receiver]) // 2
    margin = jnp.where((donor == order[0]) | (receiver == order[0]) | (sizes[receiver] == 0), 0, jnp.maximum(margin, 0))
    passed = jax.random.randint(jax.random.fold_in(own, 4), (count // 2,), 0, 1 << 20) % (margin + 1)
    sizes = sizes.at[donor].add(-passed).at[receiver].add(passed)
    members = jnp.searchsorted(jnp.cumsum(sizes), jnp.arange(rows * top), side="right").astype(jnp.int32)
    table = members.reshape(top, rows).T
    table = table[jax.random.permutation(jax.random.fold_in(own, 1), rows)]
    rotation = jax.random.randint(jax.random.fold_in(own, 2), (rows, 1), 0, top)
    return jnp.take_along_axis(table, (jnp.arange(top)[None, :] + rotation) % top, axis=1)


def shares(amount, total, limit, lean, full):
    portions = [(1 << 20) // math.isqrt(standing ** lean) + 1 for standing in range(1, amount + 1)]
    largest = limit if full else min(limit, max(-(-total // amount), total * portions[0] // sum(portions)))
    least = 1 if total - largest >= amount - 1 else 0
    holding, surplus = [largest] + [least] * (amount - 1), total - largest - least * (amount - 1)
    while surplus > 0:
        movable = [i for i in range(1, amount) if holding[i] < largest] or [i for i in range(1, amount) if holding[i] < limit]
        whole, left = sum([portions[i] for i in movable]), surplus
        for i in movable:
            extra = min(limit - holding[i], max(1, left * portions[i] // whole), surplus)
            holding[i] = holding[i] + extra
            surplus = surplus - extra
    return np.array(holding)


def centred(rng, extent, scale, most, split=(), held_as=jnp.bfloat16):
    gain = level_of(rng, extent, split, -0.22, 0.18) if split else 1.0
    result = jax.random.normal(rng, extent, jnp.float32) * scale * gain
    return jnp.minimum(jnp.maximum(result, -most), most).astype(held_as)


def setup_inputs(seed: int = 0) -> dict:
    seeds = jax.random.split(jax.random.key(seed), 8)
    tokens = centred(seeds[0], (TOKENS, D), 1.0, 6.0, ((0, 16),))
    cotangent = centred(seeds[1], (TOKENS, D), 1.0, 6.0, ((0, 16),))
    routes_keys = jax.random.split(jax.random.fold_in(seeds[2], 1), TOKENS // TOK_DEV)
    routes_turns = jax.random.permutation(jax.random.fold_in(seeds[2], 3), TOKENS // TOK_DEV)
    routes = jax.vmap(lambda own, number: deal_out(jax.random.fold_in(seeds[2], 2), own, number, TOK_DEV, EXPERTS, TOPK, CAP, 2))(routes_keys, routes_turns).reshape((TOKENS, TOPK))
    gates = jnp.clip(jnp.exp(math.log(1.0) - 2.9957323 * jax.random.uniform(seeds[3], (TOKENS, TOPK), jnp.float32) ** level_of(seeds[3], (TOKENS, TOPK), ((0, 16),), -0.2, 0.2)), 0.05, 1.0)
    gate_weight = centred(seeds[4], (EXPERTS, D, FF), D ** -0.5, 0.125, ((0, 4), (2, 2)))
    up_weight = centred(seeds[5], (EXPERTS, D, FF), D ** -0.5, 0.125, ((0, 4), (2, 2)))
    down_weight = centred(seeds[6], (EXPERTS, FF, D), FF ** -0.5, 0.21875, ((0, 4), (1, 2)))
    return {"tokens": tokens, "cotangent": cotangent, "routes": routes, "gates": gates, "gate_weight": gate_weight, "up_weight": up_weight, "down_weight": down_weight}


def slot_ranks(block_routes):
    one_hot = (block_routes[:, None] == jnp.arange(EXPERTS, dtype=jnp.int32)[None, :]).astype(jnp.int32)
    earlier = jnp.cumsum(one_hot, axis=0) - one_hot
    return jnp.sum(earlier * one_hot, axis=1).astype(jnp.int32)


def replica_sum(left, right):
    left_groups = left.reshape(N_EXPERT, N_REPLICA, CAP, left.shape[1]).astype(jnp.float32)
    right_groups = right.reshape(N_EXPERT, N_REPLICA, CAP, right.shape[1]).astype(jnp.float32)
    partial_value = jnp.einsum("srca,srcb->rab", left_groups, right_groups).astype(jnp.bfloat16)
    partial_value = lax.optimization_barrier(partial_value)
    return jnp.sum(partial_value.astype(jnp.float32), axis=0).astype(jnp.bfloat16)


def reference(tokens, cotangent, routes, gates, gate_weight, up_weight, down_weight):
    blocks = N_EXPERT * N_REPLICA
    slots_all = blocks * CAP
    per_block = routes.reshape(blocks, TOK_DEV * TOPK)
    slot_rank = jax.vmap(slot_ranks)(per_block)
    block_ids = jnp.arange(blocks, dtype=jnp.int32)[:, None]
    position = (block_ids * CAP + slot_rank).reshape(-1).astype(jnp.int32)
    chosen = routes.reshape(-1).astype(jnp.int32)
    pair_ids = jnp.arange(chosen.shape[0], dtype=jnp.int32)
    row_table = jnp.zeros((EXPERTS, slots_all), jnp.int32).at[chosen, position].set(pair_ids)
    live_table = jnp.zeros((EXPERTS, slots_all), jnp.int32).at[chosen, position].set(1)
    flat_gates = gates.reshape(-1)
    half = FF // N_TENSOR

    def one_expert(grad_total, packed):
        row_ids, live_rows, w_gate, w_up, w_down = packed
        token_ids = (row_ids // TOPK).astype(jnp.int32)
        keep = live_rows[:, None] > 0
        in_rows = jnp.where(keep, tokens[token_ids], jnp.zeros((), tokens.dtype))
        gain_rows = jnp.where(live_rows > 0, flat_gates[row_ids], jnp.zeros((), flat_gates.dtype))
        cot_rows = (gain_rows[:, None].astype(jnp.float32) * cotangent[token_ids].astype(jnp.float32)).astype(jnp.bfloat16)
        gate_parts = []
        up_parts = []
        down_parts = []
        slot_total = jnp.zeros((slots_all, D), jnp.float32)
        for half_index in range(N_TENSOR):
            col_start = half_index * half
            gate_cols = w_gate[:, col_start:col_start + half]
            up_cols = w_up[:, col_start:col_start + half]
            down_rows = w_down[col_start:col_start + half, :]
            gate_pre = jnp.dot(in_rows, gate_cols, preferred_element_type=jnp.float32)
            up_proj = jnp.dot(in_rows, up_cols, preferred_element_type=jnp.float32)
            hidden_grad = jnp.dot(cot_rows, down_rows.T, preferred_element_type=jnp.float32)
            sig_gate = jax.nn.sigmoid(gate_pre)
            activated = gate_pre * sig_gate
            hidden = (activated * up_proj).astype(jnp.bfloat16)
            gate_grad = (hidden_grad * up_proj * sig_gate * (1.0 + gate_pre * (1.0 - sig_gate))).astype(jnp.bfloat16)
            up_grad = (hidden_grad * activated).astype(jnp.bfloat16)
            row_grads = (jnp.dot(gate_grad, gate_cols.T, preferred_element_type=jnp.float32)
                         + jnp.dot(up_grad, up_cols.T, preferred_element_type=jnp.float32)).astype(jnp.bfloat16)
            slot_total = slot_total + row_grads.astype(jnp.float32)
            gate_parts.append(replica_sum(in_rows, gate_grad))
            up_parts.append(replica_sum(in_rows, up_grad))
            down_parts.append(replica_sum(hidden, cot_rows))
        slot_grads = slot_total.astype(jnp.bfloat16)
        grad_total = grad_total.at[token_ids].add(slot_grads.astype(jnp.float32))
        return grad_total, (jnp.concatenate(gate_parts, axis=1), jnp.concatenate(up_parts, axis=1),
                            jnp.concatenate(down_parts, axis=0))

    start_total = jnp.zeros((TOKENS, D), jnp.float32)
    grad_total, stacked = lax.scan(one_expert, start_total,
                                   (row_table, live_table, gate_weight, up_weight, down_weight))
    return grad_total.astype(jnp.bfloat16), stacked[0], stacked[1], stacked[2]
```

```python
import functools

import jax
import jax.numpy as jnp
from jax import lax
from jax.experimental import pallas as pl
from jax.experimental.pallas import tpu as pltpu
from jax.sharding import PartitionSpec as P

AXES = ("expert", "replica", "tensor")
VMEM_LIMIT = 58 * 1024 * 1024
ARRIVAL = ((0, 1, 2, 3), (0, 2, 1, 3))
LAST = (((1,), (1,)), ((), ()))


def permutation(sizes, target):
    n_e, n_r, n_t = sizes
    pairs = []
    for e in range(n_e):
        for r in range(n_r):
            for t in range(n_t):
                te, tr, tt = target(e, r, t)
                pairs.append(((e * n_r + r) * n_t + t, (te * n_r + tr) * n_t + tt))
    return pairs


def pick_kernel(ids, gate, up, down, w_in, w_down, sem):
    half = gate.shape[2]
    copies = [
        pltpu.make_async_copy(gate.at[ids[2]], w_in.at[:, pl.ds(0, half)], sem.at[0]),
        pltpu.make_async_copy(up.at[ids[2]], w_in.at[:, pl.ds(half, half)], sem.at[1]),
        pltpu.make_async_copy(down.at[ids[2]], w_down, sem.at[2]),
    ]
    for copy in copies:
        copy.start()
    for copy in copies:
        copy.wait()


def weights(ids, gate, up, down):
    _, width, half = gate.shape
    vmem = pl.BlockSpec(memory_space=pltpu.VMEM)
    return pl.pallas_call(
        pick_kernel,
        out_shape=(
            jax.ShapeDtypeStruct((width, 2 * half), jnp.bfloat16),
            jax.ShapeDtypeStruct((half, width), jnp.bfloat16),
        ),
        in_specs=[pl.BlockSpec(memory_space=pltpu.SMEM)]
        + [pl.BlockSpec(memory_space=pl.ANY)] * 3,
        out_specs=(vmem, vmem),
        scratch_shapes=[pltpu.SemaphoreType.DMA((3,))],
        compiler_params=pltpu.CompilerParams(vmem_limit_bytes=VMEM_LIMIT),
        name="pick",
    )(ids, gate, up, down)


def chunk_kernel(n_exp, ids, mine, other, w_in, w_down, *refs):
    keep, going, grads_t, hidden_t, pre, back = refs
    rows = mine.shape[0] // 4
    half = w_down.shape[0]
    width = w_in.shape[0]
    half_width = width // 2
    lanes = mine.shape[1] - width
    lane = lax.broadcasted_iota(jnp.int32, (rows, lanes), 1)
    mask = (lane == ids[1]) | (lane == ids[1] + n_exp)

    def run(t):
        x_ref, c_ref = (mine, other) if t == 0 else (other, mine)
        pre[...] = jnp.dot(x_ref[:, :width], w_in[...], preferred_element_type=jnp.float32)
        back[...] = lax.dot_general(
            c_ref[:, :width], w_down[...], LAST, preferred_element_type=jnp.float32
        )
        pieces = []
        for i in range(4):
            at = ARRIVAL[1].index(i)
            here, there = pl.ds(i * rows, rows), pl.ds(at * rows, rows)
            g = jnp.where(mask, x_ref[here, width:].astype(jnp.float32), 0.0)
            g = jnp.sum(g, axis=1, keepdims=True)
            gate_pre, up_proj = pre[here, :half], pre[here, half:]
            hidden_grad = g * back[there, :]
            sig = 1.0 / (1.0 + jnp.exp(-gate_pre))
            act = gate_pre * sig
            up_grad = hidden_grad * act
            gate_grad = hidden_grad * up_proj * sig * (1.0 + gate_pre * (1.0 - sig))
            hidden = g * (act * up_proj)
            grads_t[:half, here] = gate_grad.T.astype(jnp.bfloat16)
            grads_t[half:, here] = up_grad.T.astype(jnp.bfloat16)
            hidden_t[:, there] = hidden.T.astype(jnp.bfloat16)
            pieces.append(
                jnp.concatenate(
                    [gate_grad.astype(jnp.bfloat16), up_grad.astype(jnp.bfloat16)], axis=1
                )
            )
        grads = jnp.concatenate(pieces, axis=0)
        for h in range(2):
            part = lax.dot_general(
                grads,
                w_in[h * half_width : (h + 1) * half_width, :],
                LAST,
                preferred_element_type=jnp.float32,
            ).astype(jnp.bfloat16)
            out = keep if h == t else going
            for i in range(4):
                at = ARRIVAL[h].index(i)
                out[at * rows : (at + 1) * rows, :] = part[i * rows : (i + 1) * rows, :]

    @pl.when(ids[0] == 0)
    def _():
        run(0)

    @pl.when(ids[0] == 1)
    def _():
        run(1)


def chunk(ids, mine, other, n_exp, w_in, w_down):
    n, width = mine.shape[0], w_in.shape[0]
    half = w_down.shape[0]
    vmem = pl.BlockSpec(memory_space=pltpu.VMEM)
    bf16 = jnp.bfloat16
    return pl.pallas_call(
        functools.partial(chunk_kernel, n_exp),
        out_shape=(
            jax.ShapeDtypeStruct((n, width // 2), bf16),
            jax.ShapeDtypeStruct((n, width // 2), bf16),
            jax.ShapeDtypeStruct((2 * half, n), bf16),
            jax.ShapeDtypeStruct((half, n), bf16),
        ),
        in_specs=[pl.BlockSpec(memory_space=pltpu.SMEM)]
        + [vmem] * 4,
        out_specs=(vmem,) * 4,
        scratch_shapes=[
            pltpu.VMEM((n, 2 * half), jnp.float32),
            pltpu.VMEM((n, half), jnp.float32),
        ],
        compiler_params=pltpu.CompilerParams(vmem_limit_bytes=VMEM_LIMIT),
        cost_estimate=pl.CostEstimate(flops=1, bytes_accessed=1, transcendentals=0),
        name="chunk",
    )(ids, mine, other, w_in, w_down)


def weight_kernel(k, first, last, ids, *refs):
    mine, other, grads_t, hidden_t = (refs[i * k : (i + 1) * k] for i in range(4))
    refs = refs[4 * k :]
    if not first:
        had_in, had_down = refs[:2]
        refs = refs[2:]
    if last:
        gate_out, up_out, down_out = refs[:3]
        refs = refs[3:]
    else:
        acc_in, acc_down = refs[:2]
        refs = refs[2:]
    x_buf, c_buf, x_sem, c_sem = refs[:4]
    if last:
        acc_in, acc_down = refs[4:]

    def fetch(j, start):
        for t in range(2):

            @pl.when(ids[0] == t)
            def _():
                x, c = (mine, other) if t == 0 else (other, mine)
                for src, buf, sem in ((x, x_buf, x_sem), (c, c_buf, c_sem)):
                    copy = pltpu.make_async_copy(
                        src[j].at[:, pl.ds(0, buf.shape[2])], buf.at[j], sem.at[j]
                    )
                    copy.start() if start else copy.wait()

    for j in range(k):
        fetch(j, True)
    for j in range(k):
        fetch(j, False)
        part_in = jnp.dot(grads_t[j][...], x_buf[j], preferred_element_type=jnp.float32)
        part_down = jnp.dot(hidden_t[j][...], c_buf[j], preferred_element_type=jnp.float32)
        if j:
            acc_in[...] += part_in
            acc_down[...] += part_down
        elif first:
            acc_in[...] = part_in
            acc_down[...] = part_down
        else:
            acc_in[...] = had_in[...] + part_in
            acc_down[...] = had_down[...] + part_down
    if last:
        half = acc_down.shape[0]
        gate_out[0] = acc_in[:half, :].T.astype(jnp.bfloat16)
        up_out[0] = acc_in[half:, :].T.astype(jnp.bfloat16)
        down_out[0] = acc_down[...].astype(jnp.bfloat16)


def weight_grads(ids, width, mine, other, grads_t, hidden_t, had, last):
    k = len(mine)
    n, half = mine[0].shape[0], hidden_t[0].shape[0]
    vmem = pl.BlockSpec(memory_space=pltpu.VMEM)
    hbm = pl.BlockSpec(memory_space=pl.ANY)
    bf16 = jnp.bfloat16
    sums = ((2 * half, width), (half, width))
    if last:
        outs = tuple(
            jax.ShapeDtypeStruct(shape, bf16)
            for shape in ((1, width, half), (1, width, half), (1, half, width))
        )
    else:
        outs = tuple(jax.ShapeDtypeStruct(shape, jnp.float32) for shape in sums)
    scratch = [
        pltpu.VMEM((k, n, width), bf16),
        pltpu.VMEM((k, n, width), bf16),
        pltpu.SemaphoreType.DMA((k,)),
        pltpu.SemaphoreType.DMA((k,)),
    ]
    if last:
        scratch += [pltpu.VMEM(shape, jnp.float32) for shape in sums]
    return pl.pallas_call(
        functools.partial(weight_kernel, k, not had, last),
        out_shape=outs,
        in_specs=[pl.BlockSpec(memory_space=pltpu.SMEM)]
        + [hbm] * (2 * k)
        + [vmem] * (2 * k + len(had)),
        out_specs=(vmem,) * len(outs),
        scratch_shapes=scratch,
        compiler_params=pltpu.CompilerParams(vmem_limit_bytes=VMEM_LIMIT),
        cost_estimate=pl.CostEstimate(flops=1, bytes_accessed=1, transcendentals=0),
        name="weight_grads",
    )(ids, *mine, *other, *grads_t, *hidden_t, *had)


def body(tokens, cotangent, routes, gates, gate_weight, up_weight, down_weight):
    rows, width = tokens.shape
    exp_local = gate_weight.shape[0]
    sizes = tuple(lax.axis_size(a) for a in AXES)
    n_e, n_r, n_t = sizes
    assert n_r == 4 and n_t == 2 and exp_local == n_r
    e, r, t = (lax.axis_index(a) for a in AXES)
    n_exp = exp_local * n_e

    def send(x, target):
        return lax.ppermute(x, AXES, permutation(sizes, target))

    plane_a = lambda e, r, t: (e, r ^ (1 + t), t)
    plane_b = lambda e, r, t: (e, r ^ (2 - t), t)
    core = lambda e, r, t: (e, r, 1 - t)
    shift = lambda s: lambda e, r, t: ((e + s) % n_e, r, t)

    def add(a, b):
        return (a.astype(jnp.float32) + b.astype(jnp.float32)).astype(jnp.bfloat16)

    def after(x, *deps):
        return lax.optimization_barrier((x, *deps))[0]

    first_core = t == 0
    order = [0] + sorted(range(1, n_e), key=lambda s: min(s, n_e - s))

    named = routes[:, :, None] == jnp.arange(n_exp, dtype=jnp.int32)[None, None, :]
    dense = jnp.sum(jnp.where(named, gates[:, :, None], 0.0), axis=1)
    coarse = lax.reduce_precision(dense, 8, 7)
    beside = jnp.concatenate([coarse, dense - coarse], axis=1).astype(jnp.bfloat16)
    beside = jnp.pad(beside, ((0, 0), (0, -2 * n_exp % 128)))
    mine = jnp.where(first_core, tokens, cotangent)
    mine = jnp.concatenate([mine, beside], axis=1)
    expert = (e * exp_local + r).astype(jnp.int32)
    ids = jnp.stack([t.astype(jnp.int32), expert, r.astype(jnp.int32)])
    w_in, w_down = weights(ids, gate_weight, up_weight, down_weight)

    n = n_e
    plane, sent_a = [None] * n, [None] * n
    two, four, other, done, summed = ([None] * n for _ in range(5))
    groups, begin = [], 0
    while begin < n:
        stop = min(begin + 3, n - 1) if begin < n - 1 else n
        groups.append(range(begin, stop))
        begin = stop

    plane[0] = mine
    for i in range(1, n):
        plane[i] = send(mine if i == 1 else after(mine, plane[i - 1]), shift(-order[i]))

    def make_two(i, *deps):
        two[i] = after(jnp.concatenate([plane[i], send(plane[i], plane_a)]), *deps)

    make_two(0)
    had = ()
    for i in range(n):
        if i + 1 < n:
            deps = () if i < 2 else (done[i - 2][0],)
            make_two(i + 1, *deps)
        arrived = send(two[i], plane_b)
        if i + 1 < n:
            arrived = after(arrived, two[i + 1], w_in, w_down)
        four[i] = jnp.concatenate([two[i], arrived])
        other[i] = send(four[i], core)
        four_i = four[i]
        if i >= 1:
            four_i = after(four_i, summed[i - 1])
        if i == n - 1 and had:
            four_i = after(four_i, *had)
        done[i] = chunk(ids, four_i, other[i], n_exp, w_in, w_down)
        summed[i] = add(done[i][0], send(done[i][1], core))
        for group in groups:
            if group[-1] == i:
                had = weight_grads(
                    ids,
                    width,
                    [four[j] for j in group],
                    [other[j] for j in group],
                    [done[j][2] for j in group],
                    [done[j][3] for j in group],
                    had,
                    i == n - 1,
                )

    total = None
    for i, s in enumerate(order):
        keep = summed[i]
        if i + 2 == n:
            keep = after(keep, two[i + 1])
        elif i + 2 < n:
            keep = after(keep, four[i + 2])
        keep = add(keep[: 2 * rows], send(keep[2 * rows :], plane_b))
        keep = add(keep[:rows], send(keep[rows:], plane_a))
        back = keep if s == 0 else send(keep, shift(s))
        back = back.astype(jnp.float32)
        total = back if total is None else total + back
    return (total.astype(jnp.bfloat16), *had)


def solution(mesh):
    in_specs = (
        P(("expert", "replica"), None),
        P(("expert", "replica"), None),
        P(("expert", "replica"), None),
        P(("expert", "replica"), None),
        P("expert", None, "tensor"),
        P("expert", None, "tensor"),
        P("expert", "tensor", None),
    )
    out_specs = (
        P(("expert", "replica"), "tensor"),
        P(("expert", "replica"), None, "tensor"),
        P(("expert", "replica"), None, "tensor"),
        P(("expert", "replica"), "tensor", None),
    )
    return jax.shard_map(body, mesh=mesh, in_specs=in_specs, out_specs=out_specs, check_vma=False)
```

```python
import functools

import jax
import jax.numpy as jnp
from jax import lax
from jax.experimental import pallas as pl
from jax.experimental.pallas import tpu as pltpu
from jax.sharding import PartitionSpec as P

AXES = ("expert", "replica", "tensor")
PICK_LIMIT = 58 * 1024 * 1024
CHUNK_LIMIT = 26 * 1024 * 1024
WEIGHT_LIMIT = 26 * 1024 * 1024
ARRIVAL = ((0, 1, 2, 3), (0, 2, 1, 3))
LAST = (((1,), (1,)), ((), ()))


def permutation(sizes, target):
    n_e, n_r, n_t = sizes
    pairs = []
    for e in range(n_e):
        for r in range(n_r):
            for t in range(n_t):
                te, tr, tt = target(e, r, t)
                pairs.append(((e * n_r + r) * n_t + t, (te * n_r + tr) * n_t + tt))
    return pairs


def pick_kernel(ids, gate, up, down, w_in, w_down, sem):
    half = gate.shape[2]
    copies = [
        pltpu.make_async_copy(gate.at[ids[2]], w_in.at[:, pl.ds(0, half)], sem.at[0]),
        pltpu.make_async_copy(up.at[ids[2]], w_in.at[:, pl.ds(half, half)], sem.at[1]),
        pltpu.make_async_copy(down.at[ids[2]], w_down, sem.at[2]),
    ]
    for copy in copies:
        copy.start()
    for copy in copies:
        copy.wait()


def weights(ids, gate, up, down):
    _, width, half = gate.shape
    vmem = pl.BlockSpec(memory_space=pltpu.VMEM)
    return pl.pallas_call(
        pick_kernel,
        out_shape=(
            jax.ShapeDtypeStruct((width, 2 * half), jnp.bfloat16),
            jax.ShapeDtypeStruct((half, width), jnp.bfloat16),
        ),
        in_specs=[pl.BlockSpec(memory_space=pltpu.SMEM)]
        + [pl.BlockSpec(memory_space=pl.ANY)] * 3,
        out_specs=(vmem, vmem),
        scratch_shapes=[pltpu.SemaphoreType.DMA((3,))],
        compiler_params=pltpu.CompilerParams(vmem_limit_bytes=PICK_LIMIT),
        name="pick",
    )(ids, gate, up, down)


def chunk_kernel(n_exp, ids, mine_lo, mine_hi, other_lo, other_hi, w_in, w_down, *refs):
    keep, going, gate_t, up_t, hidden_t, pre, back = refs
    rows = mine_lo.shape[0] // 2
    half = w_down.shape[0]
    width = w_in.shape[0]
    half_width = width // 2
    lanes = mine_lo.shape[1] - width
    lane = lax.broadcasted_iota(jnp.int32, (rows, lanes), 1)
    mask = (lane == ids[1]) | (lane == ids[1] + n_exp)

    def run(t):
        mine, other = (mine_lo, mine_hi), (other_lo, other_hi)
        xs, cs = (mine, other) if t == 0 else (other, mine)
        for h in range(2):
            both = pl.ds(2 * h * rows, 2 * rows)
            pre[both, :] = jnp.dot(
                xs[h][:, :width], w_in[...], preferred_element_type=jnp.float32
            )
            back[both, :] = lax.dot_general(
                cs[h][:, :width], w_down[...], LAST, preferred_element_type=jnp.float32
            )
        pieces = []
        for i in range(4):
            at = ARRIVAL[1].index(i)
            here, there = pl.ds(i * rows, rows), pl.ds(at * rows, rows)
            g = xs[i // 2][pl.ds(i % 2 * rows, rows), width:].astype(jnp.float32)
            g = jnp.sum(jnp.where(mask, g, 0.0), axis=1, keepdims=True)
            gate_pre, up_proj = pre[here, :half], pre[here, half:]
            hidden_grad = g * back[there, :]
            sig = 1.0 / (1.0 + jnp.exp(-gate_pre))
            act = gate_pre * sig
            up_grad = hidden_grad * act
            gate_grad = hidden_grad * up_proj * sig * (1.0 + gate_pre * (1.0 - sig))
            hidden = g * (act * up_proj)
            gate_t[:, here] = gate_grad.T.astype(jnp.bfloat16)
            up_t[:, here] = up_grad.T.astype(jnp.bfloat16)
            hidden_t[:, there] = hidden.T.astype(jnp.bfloat16)
            pieces.append(
                jnp.concatenate(
                    [gate_grad.astype(jnp.bfloat16), up_grad.astype(jnp.bfloat16)], axis=1
                )
            )
        grads = jnp.concatenate(pieces, axis=0)
        for h in range(2):
            part = lax.dot_general(
                grads,
                w_in[h * half_width : (h + 1) * half_width, :],
                LAST,
                preferred_element_type=jnp.float32,
            ).astype(jnp.bfloat16)
            out = keep if h == t else going
            for i in range(4):
                at = ARRIVAL[h].index(i)
                out[at * rows : (at + 1) * rows, :] = part[i * rows : (i + 1) * rows, :]

    @pl.when(ids[0] == 0)
    def _():
        run(0)

    @pl.when(ids[0] == 1)
    def _():
        run(1)


def chunk(ids, mine, other, n_exp, w_in, w_down):
    n, width = 2 * mine[0].shape[0], w_in.shape[0]
    half = w_down.shape[0]
    vmem = pl.BlockSpec(memory_space=pltpu.VMEM)
    bf16 = jnp.bfloat16
    return pl.pallas_call(
        functools.partial(chunk_kernel, n_exp),
        out_shape=(
            jax.ShapeDtypeStruct((n, width // 2), bf16),
            jax.ShapeDtypeStruct((n, width // 2), bf16),
            jax.ShapeDtypeStruct((half, n), bf16),
            jax.ShapeDtypeStruct((half, n), bf16),
            jax.ShapeDtypeStruct((half, n), bf16),
        ),
        in_specs=[pl.BlockSpec(memory_space=pltpu.SMEM)]
        + [vmem] * 6,
        out_specs=(vmem,) * 5,
        scratch_shapes=[
            pltpu.VMEM((n, 2 * half), jnp.float32),
            pltpu.VMEM((n, half), jnp.float32),
        ],
        compiler_params=pltpu.CompilerParams(vmem_limit_bytes=CHUNK_LIMIT),
        cost_estimate=pl.CostEstimate(flops=1, bytes_accessed=1, transcendentals=0),
        name="chunk",
    )(ids, *mine, *other, w_in, w_down)


def weight_kernel(k, swap, carried, ids, *refs):
    mine, other, left = refs[: 2 * k], refs[2 * k : 4 * k], refs[4 * k : 5 * k]
    refs = refs[5 * k :]
    if carried:
        had, refs = refs[0], refs[1:]
    out, buf, sem = refs
    n = buf.shape[1] // 2

    def fetch(j, start):
        for t in range(2):

            @pl.when(ids[0] == t)
            def _():
                src = mine if (t == 1) == swap else other
                for h in range(2):
                    copy = pltpu.make_async_copy(
                        src[2 * j + h].at[:, pl.ds(0, buf.shape[2])],
                        buf.at[j, pl.ds(h * n, n)],
                        sem.at[j, h],
                    )
                    copy.start() if start else copy.wait()

    for j in range(k):
        fetch(j, True)
    total = None
    for j in range(k):
        fetch(j, False)
        part = jnp.dot(left[j][...], buf[j], preferred_element_type=jnp.float32)
        total = part if total is None else total + part
    total = total if swap else total.T
    if carried:
        total = total + had[0].astype(jnp.float32)
    out[0] = total.astype(out.dtype)


def weight_grad(ids, width, mine, other, left, had, swap, dtype):
    k, n, half = len(left), 2 * mine[0][0].shape[0], left[0].shape[0]
    vmem = pl.BlockSpec(memory_space=pltpu.VMEM)
    return pl.pallas_call(
        functools.partial(weight_kernel, k, swap, len(had)),
        out_shape=jax.ShapeDtypeStruct((1, half, width) if swap else (1, width, half), dtype),
        in_specs=[pl.BlockSpec(memory_space=pltpu.SMEM)]
        + [pl.BlockSpec(memory_space=pl.ANY)] * (4 * k)
        + [vmem] * (k + len(had)),
        out_specs=vmem,
        scratch_shapes=[
            pltpu.VMEM((k, n, width), jnp.bfloat16),
            pltpu.SemaphoreType.DMA((k, 2)),
        ],
        compiler_params=pltpu.CompilerParams(vmem_limit_bytes=WEIGHT_LIMIT),
        name="weight_grad",
    )(ids, *[h for m in mine for h in m], *[h for o in other for h in o], *left, *had)


def body(tokens, cotangent, routes, gates, gate_weight, up_weight, down_weight):
    rows, width = tokens.shape
    exp_local = gate_weight.shape[0]
    sizes = tuple(lax.axis_size(a) for a in AXES)
    n_e, n_r, n_t = sizes
    assert n_e >= 4 and n_r == 4 and n_t == 2 and exp_local == n_r
    e, r, t = (lax.axis_index(a) for a in AXES)
    n_exp = exp_local * n_e

    def send(x, target):
        return lax.ppermute(x, AXES, permutation(sizes, target))

    plane_a = lambda e, r, t: (e, r ^ (1 + t), t)
    plane_b = lambda e, r, t: (e, r ^ (2 - t), t)
    core = lambda e, r, t: (e, r, 1 - t)
    shift = lambda s: lambda e, r, t: ((e + s) % n_e, r, t)

    def add(a, b):
        return (a.astype(jnp.float32) + b.astype(jnp.float32)).astype(jnp.bfloat16)

    def after(x, *deps):
        return lax.optimization_barrier((x, *deps))[0]

    first_core = t == 0

    named = routes[:, :, None] == jnp.arange(n_exp, dtype=jnp.int32)[None, None, :]
    dense = jnp.sum(jnp.where(named, gates[:, :, None], 0.0), axis=1)
    coarse = lax.reduce_precision(dense, 8, 7)
    beside = jnp.concatenate([coarse, dense - coarse], axis=1).astype(jnp.bfloat16)
    beside = jnp.pad(beside, ((0, 0), (0, -2 * n_exp % 128)))
    mine = jnp.where(first_core, tokens, cotangent)
    mine = jnp.concatenate([mine, beside], axis=1)
    expert = (e * exp_local + r).astype(jnp.int32)
    ids = jnp.stack([t.astype(jnp.int32), expert, r.astype(jnp.int32)])
    w_in, w_down = weights(ids, gate_weight, up_weight, down_weight)

    n = n_e
    last = n - 1
    plane, two, sent_b, mine_of, other_of, done = ([None] * n for _ in range(6))
    summed, half_way, most = ([None] * n for _ in range(3))

    def grad(chunks, at, had, *deps):
        swap = at == 4
        total = None
        for begin in range(0, len(chunks), 4):
            group = chunks[begin : begin + 4]
            part = weight_grad(
                after(ids, *deps),
                width,
                [mine_of[j] for j in group],
                [other_of[j] for j in group],
                [done[j][at] for j in group],
                had,
                swap,
                jnp.bfloat16 if len(chunks) <= 4 else jnp.float32,
            )
            total = part if total is None else total + part
        return total.astype(jnp.bfloat16)

    early, late = range(n - 2), range(n - 2, n)

    plane[0] = mine
    plane[1] = send(mine, shift(-1))
    two[0] = after(jnp.concatenate([mine, send(mine, plane_a)]), w_in, w_down)
    sent_b[0] = send(two[0], plane_b)
    came_lo = send(two[0], core)
    came_a = send(plane[1], plane_a)
    plane[2] = send(plane[1], shift(-1))
    two[1] = after(jnp.concatenate([plane[1], came_a]), plane[2], came_lo)

    home = {}
    for i in range(1, n + 1):
        beside = {}
        if i < n:
            sent_b[i] = send(two[i], plane_b)
        if i + 1 < n:
            beside["a"] = send(plane[i + 1], plane_a)
        if i + 2 < n:
            beside["z"] = send(plane[i + 1], shift(-1))
        if i >= 2:
            came_core = send(done[i - 2][1], core)
        if i >= 4:
            beside["home"] = send(half_way[i - 3][rows:], plane_a)
        if i >= 5:
            home[i - 4] = send(most[i - 4], shift(i - 4))
        arrived = sent_b[i - 1]
        if i < n:
            arrived = after(arrived, two[i])
        else:
            gate_had = grad(early, 2, (), done[i - 2][0])
            arrived = after(arrived, gate_had)
        mine_of[i - 1] = (two[i - 1], arrived)
        came_hi = send(arrived, core)
        if i >= 2:
            summed[i - 2] = add(done[i - 2][0], came_core)
            came_hi = after(came_hi, summed[i - 2])
        if i >= 3:
            beside["b"] = send(summed[i - 2][2 * rows :], plane_b)
        if i == n - 1:
            down_had = grad(early, 4, (), two[i])
            came_hi = after(came_hi, down_had)
        if i == n:
            up_had = grad(early, 3, (), arrived)
            came_hi = after(came_hi, up_had)
        if i < n:
            beside["lo"] = send(two[i], core)
        other_of[i - 1] = (came_lo, came_hi)
        done[i - 1] = chunk(ids, mine_of[i - 1], other_of[i - 1], n_exp, w_in, w_down)
        beside, done[i - 1], summed[i - 2] = lax.optimization_barrier(
            (beside, done[i - 1], summed[i - 2])
        )
        came_lo = beside.get("lo")
        if i + 1 < n:
            two[i + 1] = jnp.concatenate([plane[i + 1], beside["a"]])
        if i + 2 < n:
            plane[i + 2] = beside["z"]
        if i >= 3:
            half_way[i - 2] = add(summed[i - 2][: 2 * rows], beside["b"])
        if i >= 4:
            most[i - 3] = add(half_way[i - 3][:rows], beside["home"])

    came_core = send(done[last][1], core)
    came_home = send(half_way[n - 2][rows:], plane_a)
    came_b = send(summed[0][2 * rows :], plane_b)
    home[n - 3] = send(most[n - 3], shift(n - 3))
    down_out = grad(late, 4, (down_had,), half_way[n - 2])
    came_core, came_home, came_b, home, down_out = lax.optimization_barrier(
        (came_core, came_home, came_b, home, down_out)
    )
    most[n - 2] = add(half_way[n - 2][:rows], came_home)
    half_way[0] = add(summed[0][: 2 * rows], came_b)
    summed[last] = add(done[last][0], came_core)

    home[n - 2] = send(most[n - 2], shift(n - 2))
    came_b = send(summed[last][2 * rows :], plane_b)
    gate_out = grad(late, 2, (gate_had,), summed[last])
    came_b, gate_out = lax.optimization_barrier((came_b, gate_out))
    half_way[last] = add(summed[last][: 2 * rows], came_b)

    came_home = send(half_way[last][rows:], plane_a)
    came_home, home = lax.optimization_barrier((came_home, home))
    most[last] = add(half_way[last][:rows], came_home)

    home[last] = send(most[last], shift(last))
    most[0] = add(half_way[0][:rows], send(half_way[0][rows:], plane_a))
    up_out = grad(late, 3, (up_had,), most[last])

    total = most[0].astype(jnp.float32)
    for s in range(1, n):
        total = total + home[s].astype(jnp.float32)
    return total.astype(jnp.bfloat16), gate_out, up_out, down_out


def solution(mesh):
    in_specs = (
        P(("expert", "replica"), None),
        P(("expert", "replica"), None),
        P(("expert", "replica"), None),
        P(("expert", "replica"), None),
        P("expert", None, "tensor"),
        P("expert", None, "tensor"),
        P("expert", "tensor", None),
    )
    out_specs = (
        P(("expert", "replica"), "tensor"),
        P(("expert", "replica"), None, "tensor"),
        P(("expert", "replica"), None, "tensor"),
        P(("expert", "replica"), "tensor", None),
    )
    return jax.shard_map(body, mesh=mesh, in_specs=in_specs, out_specs=out_specs, check_vma=False)
```

```python
import functools

import jax
import jax.numpy as jnp
from jax import lax
from jax.experimental import pallas as pl
from jax.experimental.pallas import tpu as pltpu
from jax.sharding import PartitionSpec as P

AXES = ("expert", "replica", "tensor")
PICK_LIMIT = 58 * 1024 * 1024
CHUNK_LIMIT = 26 * 1024 * 1024
WEIGHT_LIMIT = 26 * 1024 * 1024
ARRIVAL = ((0, 1, 2, 3), (0, 2, 1, 3))
LAST = (((1,), (1,)), ((), ()))


def permutation(sizes, target):
    n_e, n_r, n_t = sizes
    pairs = []
    for e in range(n_e):
        for r in range(n_r):
            for t in range(n_t):
                te, tr, tt = target(e, r, t)
                pairs.append(((e * n_r + r) * n_t + t, (te * n_r + tr) * n_t + tt))
    return pairs


def pick_kernel(ids, gate, up, down, w_in, w_down, sem):
    half = gate.shape[2]
    copies = [
        pltpu.make_async_copy(gate.at[ids[2]], w_in.at[:, pl.ds(0, half)], sem.at[0]),
        pltpu.make_async_copy(up.at[ids[2]], w_in.at[:, pl.ds(half, half)], sem.at[1]),
        pltpu.make_async_copy(down.at[ids[2]], w_down, sem.at[2]),
    ]
    for copy in copies:
        copy.start()
    for copy in copies:
        copy.wait()


def weights(ids, gate, up, down):
    _, width, half = gate.shape
    vmem = pl.BlockSpec(memory_space=pltpu.VMEM)
    return pl.pallas_call(
        pick_kernel,
        out_shape=(
            jax.ShapeDtypeStruct((width, 2 * half), jnp.bfloat16),
            jax.ShapeDtypeStruct((half, width), jnp.bfloat16),
        ),
        in_specs=[pl.BlockSpec(memory_space=pltpu.SMEM)]
        + [pl.BlockSpec(memory_space=pl.ANY)] * 3,
        out_specs=(vmem, vmem),
        scratch_shapes=[pltpu.SemaphoreType.DMA((3,))],
        compiler_params=pltpu.CompilerParams(vmem_limit_bytes=PICK_LIMIT),
        name="pick",
    )(ids, gate, up, down)


def chunk_kernel(n_exp, ids, mine_lo, mine_hi, other_lo, other_hi, w_in, w_down, *refs):
    keep, going, gate_t, up_t, hidden_t, pre, back = refs
    rows = mine_lo.shape[0] // 2
    half = w_down.shape[0]
    width = w_in.shape[0]
    half_width = width // 2
    lanes = mine_lo.shape[1] - width
    lane = lax.broadcasted_iota(jnp.int32, (rows, lanes), 1)
    mask = (lane == ids[1]) | (lane == ids[1] + n_exp)

    def run(t):
        mine, other = (mine_lo, mine_hi), (other_lo, other_hi)
        xs, cs = (mine, other) if t == 0 else (other, mine)
        for h in range(2):
            both = pl.ds(2 * h * rows, 2 * rows)
            pre[both, :] = jnp.dot(
                xs[h][:, :width], w_in[...], preferred_element_type=jnp.float32
            )
            back[both, :] = lax.dot_general(
                cs[h][:, :width], w_down[...], LAST, preferred_element_type=jnp.float32
            )
        pieces = []
        for i in range(4):
            at = ARRIVAL[1].index(i)
            here, there = pl.ds(i * rows, rows), pl.ds(at * rows, rows)
            g = xs[i // 2][pl.ds(i % 2 * rows, rows), width:].astype(jnp.float32)
            g = jnp.sum(jnp.where(mask, g, 0.0), axis=1, keepdims=True)
            gate_pre, up_proj = pre[here, :half], pre[here, half:]
            hidden_grad = g * back[there, :]
            sig = 1.0 / (1.0 + jnp.exp(-gate_pre))
            act = gate_pre * sig
            up_grad = hidden_grad * act
            gate_grad = hidden_grad * up_proj * sig * (1.0 + gate_pre * (1.0 - sig))
            hidden = g * (act * up_proj)
            gate_t[:, here] = gate_grad.T.astype(jnp.bfloat16)
            up_t[:, here] = up_grad.T.astype(jnp.bfloat16)
            hidden_t[:, there] = hidden.T.astype(jnp.bfloat16)
            pieces.append(
                jnp.concatenate(
                    [gate_grad.astype(jnp.bfloat16), up_grad.astype(jnp.bfloat16)], axis=1
                )
            )
        grads = jnp.concatenate(pieces, axis=0)
        for h in range(2):
            part = lax.dot_general(
                grads,
                w_in[h * half_width : (h + 1) * half_width, :],
                LAST,
                preferred_element_type=jnp.float32,
            ).astype(jnp.bfloat16)
            out = keep if h == t else going
            for i in range(4):
                at = ARRIVAL[h].index(i)
                out[at * rows : (at + 1) * rows, :] = part[i * rows : (i + 1) * rows, :]

    @pl.when(ids[0] == 0)
    def _():
        run(0)

    @pl.when(ids[0] == 1)
    def _():
        run(1)


def chunk(ids, mine, other, n_exp, w_in, w_down):
    n, width = 2 * mine[0].shape[0], w_in.shape[0]
    half = w_down.shape[0]
    vmem = pl.BlockSpec(memory_space=pltpu.VMEM)
    bf16 = jnp.bfloat16
    return pl.pallas_call(
        functools.partial(chunk_kernel, n_exp),
        out_shape=(
            jax.ShapeDtypeStruct((n, width // 2), bf16),
            jax.ShapeDtypeStruct((n, width // 2), bf16),
            jax.ShapeDtypeStruct((half, n), bf16),
            jax.ShapeDtypeStruct((half, n), bf16),
            jax.ShapeDtypeStruct((half, n), bf16),
        ),
        in_specs=[pl.BlockSpec(memory_space=pltpu.SMEM)]
        + [vmem] * 6,
        out_specs=(vmem,) * 5,
        scratch_shapes=[
            pltpu.VMEM((n, 2 * half), jnp.float32),
            pltpu.VMEM((n, half), jnp.float32),
        ],
        compiler_params=pltpu.CompilerParams(vmem_limit_bytes=CHUNK_LIMIT),
        cost_estimate=pl.CostEstimate(flops=1, bytes_accessed=1, transcendentals=0),
        name="chunk",
    )(ids, *mine, *other, w_in, w_down)


def weight_kernel(k, swap, carried, ids, *refs):
    mine, other, left = refs[: 2 * k], refs[2 * k : 4 * k], refs[4 * k : 5 * k]
    refs = refs[5 * k :]
    if carried:
        had, refs = refs[0], refs[1:]
    out, buf, sem = refs
    n = buf.shape[1] // 2

    def fetch(j, start):
        for t in range(2):

            @pl.when(ids[0] == t)
            def _():
                src = mine if (t == 1) == swap else other
                for h in range(2):
                    copy = pltpu.make_async_copy(
                        src[2 * j + h].at[:, pl.ds(0, buf.shape[2])],
                        buf.at[j, pl.ds(h * n, n)],
                        sem.at[j, h],
                    )
                    copy.start() if start else copy.wait()

    for j in range(k):
        fetch(j, True)
    total = None
    for j in range(k):
        fetch(j, False)
        part = jnp.dot(left[j][...], buf[j], preferred_element_type=jnp.float32)
        total = part if total is None else total + part
    total = total if swap else total.T
    if carried:
        total = total + had[0].astype(jnp.float32)
    out[0] = total.astype(out.dtype)


def weight_grad(ids, width, mine, other, left, had, swap, dtype):
    k, n, half = len(left), 2 * mine[0][0].shape[0], left[0].shape[0]
    vmem = pl.BlockSpec(memory_space=pltpu.VMEM)
    return pl.pallas_call(
        functools.partial(weight_kernel, k, swap, len(had)),
        out_shape=jax.ShapeDtypeStruct((1, half, width) if swap else (1, width, half), dtype),
        in_specs=[pl.BlockSpec(memory_space=pltpu.SMEM)]
        + [pl.BlockSpec(memory_space=pl.ANY)] * (4 * k)
        + [vmem] * (k + len(had)),
        out_specs=vmem,
        scratch_shapes=[
            pltpu.VMEM((k, n, width), jnp.bfloat16),
            pltpu.SemaphoreType.DMA((k, 2)),
        ],
        compiler_params=pltpu.CompilerParams(vmem_limit_bytes=WEIGHT_LIMIT),
        name="weight_grad",
    )(ids, *[h for m in mine for h in m], *[h for o in other for h in o], *left, *had)


def body(tokens, cotangent, routes, gates, gate_weight, up_weight, down_weight):
    rows, width = tokens.shape
    exp_local = gate_weight.shape[0]
    sizes = tuple(lax.axis_size(a) for a in AXES)
    n_e, n_r, n_t = sizes
    assert n_e >= 4 and n_r == 4 and n_t == 2 and exp_local == n_r
    e, r, t = (lax.axis_index(a) for a in AXES)
    n_exp = exp_local * n_e

    def send(x, target):
        return lax.ppermute(x, AXES, permutation(sizes, target))

    plane_a = lambda e, r, t: (e, r ^ (1 + t), t)
    plane_b = lambda e, r, t: (e, r ^ (2 - t), t)
    core = lambda e, r, t: (e, r, 1 - t)
    shift = lambda s: lambda e, r, t: ((e + s) % n_e, r, t)

    def add(a, b):
        return (a.astype(jnp.float32) + b.astype(jnp.float32)).astype(jnp.bfloat16)

    def after(x, *deps):
        return lax.optimization_barrier((x, *deps))[0]

    first_core = t == 0

    named = routes[:, :, None] == jnp.arange(n_exp, dtype=jnp.int32)[None, None, :]
    dense = jnp.sum(jnp.where(named, gates[:, :, None], 0.0), axis=1)
    coarse = lax.reduce_precision(dense, 8, 7)
    beside = jnp.concatenate([coarse, dense - coarse], axis=1).astype(jnp.bfloat16)
    beside = jnp.pad(beside, ((0, 0), (0, -2 * n_exp % 128)))
    mine = jnp.where(first_core, tokens, cotangent)
    mine = jnp.concatenate([mine, beside], axis=1)
    expert = (e * exp_local + r).astype(jnp.int32)
    ids = jnp.stack([t.astype(jnp.int32), expert, r.astype(jnp.int32)])
    w_in, w_down = weights(ids, gate_weight, up_weight, down_weight)

    n = n_e
    last = n - 1
    plane, two, sent_b, mine_of, other_of, done = ([None] * n for _ in range(6))
    summed, half_way, most = ([None] * n for _ in range(3))

    def grad(chunks, at, had, *deps):
        swap = at == 4
        total = None
        for begin in range(0, len(chunks), 4):
            group = chunks[begin : begin + 4]
            part = weight_grad(
                after(ids, *deps),
                width,
                [mine_of[j] for j in group],
                [other_of[j] for j in group],
                [done[j][at] for j in group],
                had,
                swap,
                jnp.bfloat16 if len(chunks) <= 4 else jnp.float32,
            )
            total = part if total is None else total + part
        return total.astype(jnp.bfloat16)

    early, late = range(2), range(n - 2, n)
    if n > 4:
        early = range(n - 2)

    plane[0] = mine
    plane[1] = send(mine, shift(-1))
    two[0] = after(jnp.concatenate([mine, send(mine, plane_a)]), w_in, w_down)
    sent_b[0] = send(two[0], plane_b)
    came_lo = send(two[0], core)
    came_a = send(plane[1], plane_a)
    plane[2] = send(plane[1], shift(-1))
    two[1] = after(jnp.concatenate([plane[1], came_a]), plane[2], came_lo)

    home = {}
    for i in range(1, n + 1):
        beside = {}
        if i < n:
            sent_b[i] = send(two[i], plane_b)
        if i + 1 < n:
            beside["a"] = send(plane[i + 1], plane_a)
        if i + 2 < n:
            beside["z"] = send(plane[i + 1], shift(-1))
        if i >= 2:
            came_core = send(done[i - 2][1], core)
            summed[i - 2] = add(done[i - 2][0], came_core)
        if i == 3:
            beside["far"] = send(summed[1][2 * rows :], shift(1))
        if i == 4:
            beside["own"] = send(far, plane_b)
            beside["near"] = send(summed[1][: 2 * rows], shift(1))
        if i >= 4:
            beside["b"] = send(summed[i - 2][2 * rows :], plane_b)
        if i >= 5:
            beside["home"] = send(half_way[i - 3][rows:], plane_a)
        if i >= 6:
            home[i - 4] = send(most[i - 4], shift(i - 4))
        arrived = sent_b[i - 1]
        if i < n:
            arrived = after(arrived, two[i], *([summed[i - 2]] if i >= 2 else []))
        mine_of[i - 1] = (two[i - 1], arrived)
        came_hi = send(arrived, core)
        if i >= 2:
            came_hi, summed[i - 2] = lax.optimization_barrier((came_hi, summed[i - 2]))
        if i < n:
            beside["lo"] = send(two[i], core)
        other_of[i - 1] = (came_lo, came_hi)
        done[i - 1] = chunk(ids, mine_of[i - 1], other_of[i - 1], n_exp, w_in, w_down)
        if i == early[-1] + 1:
            beside["grads"] = [grad(early, at, (), done[i - 1][0]) for at in (2, 3, 4)]
        beside, done[i - 1] = lax.optimization_barrier((beside, done[i - 1]))
        if i < n:
            sent_b[i] = after(sent_b[i], done[i - 1][0])
        if i == early[-1] + 1:
            gate_had, up_had, down_had = beside["grads"]
        came_lo = beside.get("lo")
        if i + 1 < n:
            two[i + 1] = jnp.concatenate([plane[i + 1], beside["a"]])
        if i + 2 < n:
            plane[i + 2] = beside["z"]
        if i == 3:
            far = add(summed[0][2 * rows :], beside["far"])
        if i == 4:
            near = add(summed[0][: 2 * rows], beside["near"])
            came_b = beside["own"]
        if i >= 4:
            half_way[i - 2] = add(summed[i - 2][: 2 * rows], beside["b"])
        if i >= 5:
            most[i - 3] = add(half_way[i - 3][:rows], beside["home"])

    came_core = send(done[last][1], core)
    came_home = send(half_way[n - 2][rows:], plane_a)
    if n > 4:
        home[n - 3] = send(most[n - 3], shift(n - 3))
    down_out = grad(late, 4, (down_had,), half_way[n - 2])
    came_core, came_home, home, down_out = lax.optimization_barrier(
        (came_core, came_home, home, down_out)
    )
    most[n - 2] = add(half_way[n - 2][:rows], came_home)
    summed[last] = add(done[last][0], came_core)

    home[n - 2] = send(most[n - 2], shift(n - 2))
    to_b = send(summed[last][2 * rows :], plane_b)
    gate_out = grad(late, 2, (gate_had,), summed[last])
    to_b, gate_out = lax.optimization_barrier((to_b, gate_out))
    half_way[last] = add(summed[last][: 2 * rows], to_b)

    came_home = send(half_way[last][rows:], plane_a)
    came_home, home = lax.optimization_barrier((came_home, home))
    most[last] = add(half_way[last][:rows], came_home)

    home[last] = send(most[last], shift(last))
    near = add(near, came_b)
    own = after(near[rows:], half_way[last])
    own = send(own, plane_a).astype(jnp.float32)
    up_out = grad(late, 3, (up_had,), most[last])
    most[0] = own + near[:rows].astype(jnp.float32)

    total = most[0].astype(jnp.float32)
    for s in range(2, n):
        total = total + home[s].astype(jnp.float32)
    return total.astype(jnp.bfloat16), gate_out, up_out, down_out


def solution(mesh):
    in_specs = (
        P(("expert", "replica"), None),
        P(("expert", "replica"), None),
        P(("expert", "replica"), None),
        P(("expert", "replica"), None),
        P("expert", None, "tensor"),
        P("expert", None, "tensor"),
        P("expert", "tensor", None),
    )
    out_specs = (
        P(("expert", "replica"), "tensor"),
        P(("expert", "replica"), None, "tensor"),
        P(("expert", "replica"), None, "tensor"),
        P(("expert", "replica"), "tensor", None),
    )
    return jax.shard_map(body, mesh=mesh, in_specs=in_specs, out_specs=out_specs, check_vma=False)
```

```python
import functools

import jax
import jax.numpy as jnp
from jax import lax
from jax.experimental import pallas as pl
from jax.experimental.pallas import tpu as pltpu
from jax.sharding import PartitionSpec as P

AXES = ("expert", "replica", "tensor")
PICK_LIMIT = 58 * 1024 * 1024
CHUNK_LIMIT = 26 * 1024 * 1024
WEIGHT_LIMIT = 26 * 1024 * 1024
ARRIVAL = ((0, 1, 2, 3), (0, 2, 1, 3))
LAST = (((1,), (1,)), ((), ()))


def permutation(sizes, target):
    n_e, n_r, n_t = sizes
    pairs = []
    for e in range(n_e):
        for r in range(n_r):
            for t in range(n_t):
                te, tr, tt = target(e, r, t)
                pairs.append(((e * n_r + r) * n_t + t, (te * n_r + tr) * n_t + tt))
    return pairs


def pick_kernel(ids, gate, up, down, w_in, w_down, sem):
    width, half = gate.shape[1:]
    parts = sem.shape[1]
    copies = []
    for p in range(parts):
        tall, low = (pl.ds(p * (n // parts), n // parts) for n in (width, half))
        for i, (src, rows, dst) in enumerate(
            (
                (gate, tall, w_in.at[tall, pl.ds(0, half)]),
                (up, tall, w_in.at[tall, pl.ds(half, half)]),
                (down, low, w_down.at[low]),
            )
        ):
            copies.append(pltpu.make_async_copy(src.at[ids[2], rows], dst, sem.at[i, p]))
    for copy in copies:
        copy.start()
    for copy in copies:
        copy.wait()


def weights(ids, gate, up, down):
    _, width, half = gate.shape
    return pl.pallas_call(
        pick_kernel,
        out_shape=(
            jax.ShapeDtypeStruct((width, 2 * half), jnp.bfloat16),
            jax.ShapeDtypeStruct((half, width), jnp.bfloat16),
        ),
        in_specs=[pl.BlockSpec(memory_space=pltpu.SMEM)]
        + [pl.BlockSpec(memory_space=pl.ANY)] * 3,
        out_specs=(pl.BlockSpec(memory_space=pl.ANY),) * 2,
        scratch_shapes=[pltpu.SemaphoreType.DMA((3, 4))],
        compiler_params=pltpu.CompilerParams(vmem_limit_bytes=PICK_LIMIT),
        name="pick",
    )(ids, gate, up, down)


def chunk_kernel(n_exp, ids, mine_lo, mine_hi, other_lo, other_hi, w_in, w_down, *refs):
    keep, going, gate_t, up_t, hidden_t, pre, back = refs
    rows = mine_lo.shape[0] // 2
    half = w_down.shape[0]
    width = w_in.shape[0]
    half_width = width // 2
    lanes = mine_lo.shape[1] - width
    lane = lax.broadcasted_iota(jnp.int32, (rows, lanes), 1)
    mask = (lane == ids[1]) | (lane == ids[1] + n_exp)

    def run(t):
        mine, other = (mine_lo, mine_hi), (other_lo, other_hi)
        xs, cs = (mine, other) if t == 0 else (other, mine)
        for h in range(2):
            both = pl.ds(2 * h * rows, 2 * rows)
            pre[both, :] = jnp.dot(
                xs[h][:, :width], w_in[...], preferred_element_type=jnp.float32
            )
            back[both, :] = lax.dot_general(
                cs[h][:, :width], w_down[...], LAST, preferred_element_type=jnp.float32
            )
        pieces = []
        for i in range(4):
            at = ARRIVAL[1].index(i)
            here, there = pl.ds(i * rows, rows), pl.ds(at * rows, rows)
            g = xs[i // 2][pl.ds(i % 2 * rows, rows), width:].astype(jnp.float32)
            g = jnp.sum(jnp.where(mask, g, 0.0), axis=1, keepdims=True)
            gate_pre, up_proj = pre[here, :half], pre[here, half:]
            hidden_grad = g * back[there, :]
            sig = 1.0 / (1.0 + jnp.exp(-gate_pre))
            act = gate_pre * sig
            up_grad = hidden_grad * act
            gate_grad = hidden_grad * up_proj * sig * (1.0 + gate_pre * (1.0 - sig))
            hidden = g * (act * up_proj)
            gate_t[:, here] = gate_grad.T.astype(jnp.bfloat16)
            up_t[:, here] = up_grad.T.astype(jnp.bfloat16)
            hidden_t[:, there] = hidden.T.astype(jnp.bfloat16)
            pieces.append(
                jnp.concatenate(
                    [gate_grad.astype(jnp.bfloat16), up_grad.astype(jnp.bfloat16)], axis=1
                )
            )
        grads = jnp.concatenate(pieces, axis=0)
        for h in range(2):
            part = lax.dot_general(
                grads,
                w_in[h * half_width : (h + 1) * half_width, :],
                LAST,
                preferred_element_type=jnp.float32,
            ).astype(jnp.bfloat16)
            out = keep if h == t else going
            for i in range(4):
                at = ARRIVAL[h].index(i)
                out[at * rows : (at + 1) * rows, :] = part[i * rows : (i + 1) * rows, :]

    @pl.when(ids[0] == 0)
    def _():
        run(0)

    @pl.when(ids[0] == 1)
    def _():
        run(1)


def chunk(ids, mine, other, n_exp, w_in, w_down):
    n, width = 2 * mine[0].shape[0], w_in.shape[0]
    half = w_down.shape[0]
    vmem = pl.BlockSpec(memory_space=pltpu.VMEM)
    bf16 = jnp.bfloat16
    return pl.pallas_call(
        functools.partial(chunk_kernel, n_exp),
        out_shape=(
            jax.ShapeDtypeStruct((n, width // 2), bf16),
            jax.ShapeDtypeStruct((n, width // 2), bf16),
            jax.ShapeDtypeStruct((half, n), bf16),
            jax.ShapeDtypeStruct((half, n), bf16),
            jax.ShapeDtypeStruct((half, n), bf16),
        ),
        in_specs=[pl.BlockSpec(memory_space=pltpu.SMEM)]
        + [vmem] * 6,
        out_specs=(vmem,) * 5,
        scratch_shapes=[
            pltpu.VMEM((n, 2 * half), jnp.float32),
            pltpu.VMEM((n, half), jnp.float32),
        ],
        compiler_params=pltpu.CompilerParams(vmem_limit_bytes=CHUNK_LIMIT),
        cost_estimate=pl.CostEstimate(flops=1, bytes_accessed=1, transcendentals=0),
        name="chunk",
    )(ids, *mine, *other, w_in, w_down)


def weight_kernel(k, swap, carried, ids, *refs):
    mine, other, left = refs[: 2 * k], refs[2 * k : 4 * k], refs[4 * k : 5 * k]
    refs = refs[5 * k :]
    if carried:
        had, refs = refs[0], refs[1:]
    out, buf, sem = refs
    n = buf.shape[1] // 2

    def fetch(j, start):
        for t in range(2):

            @pl.when(ids[0] == t)
            def _():
                src = mine if (t == 1) == swap else other
                for h in range(2):
                    copy = pltpu.make_async_copy(
                        src[2 * j + h].at[:, pl.ds(0, buf.shape[2])],
                        buf.at[j, pl.ds(h * n, n)],
                        sem.at[j, h],
                    )
                    copy.start() if start else copy.wait()

    for j in range(k):
        fetch(j, True)
    total = None
    for j in range(k):
        fetch(j, False)
        part = jnp.dot(left[j][...], buf[j], preferred_element_type=jnp.float32)
        total = part if total is None else total + part
    total = total if swap else total.T
    if carried:
        total = total + had[0].astype(jnp.float32)
    out[0] = total.astype(out.dtype)


def weight_grad(ids, width, mine, other, left, had, swap, dtype):
    k, n, half = len(left), 2 * mine[0][0].shape[0], left[0].shape[0]
    vmem = pl.BlockSpec(memory_space=pltpu.VMEM)
    return pl.pallas_call(
        functools.partial(weight_kernel, k, swap, len(had)),
        out_shape=jax.ShapeDtypeStruct((1, half, width) if swap else (1, width, half), dtype),
        in_specs=[pl.BlockSpec(memory_space=pltpu.SMEM)]
        + [pl.BlockSpec(memory_space=pl.ANY)] * (4 * k)
        + [vmem] * (k + len(had)),
        out_specs=vmem,
        scratch_shapes=[
            pltpu.VMEM((k, n, width), jnp.bfloat16),
            pltpu.SemaphoreType.DMA((k, 2)),
        ],
        compiler_params=pltpu.CompilerParams(vmem_limit_bytes=WEIGHT_LIMIT),
        name="weight_grad",
    )(ids, *[h for m in mine for h in m], *[h for o in other for h in o], *left, *had)


def body(tokens, cotangent, routes, gates, gate_weight, up_weight, down_weight):
    rows, width = tokens.shape
    exp_local = gate_weight.shape[0]
    sizes = tuple(lax.axis_size(a) for a in AXES)
    n_e, n_r, n_t = sizes
    assert n_e >= 4 and n_r == 4 and n_t == 2 and exp_local == n_r
    e, r, t = (lax.axis_index(a) for a in AXES)
    n_exp = exp_local * n_e

    def send(x, target):
        return lax.ppermute(x, AXES, permutation(sizes, target))

    plane_a = lambda e, r, t: (e, r ^ (1 + t), t)
    plane_b = lambda e, r, t: (e, r ^ (2 - t), t)
    core = lambda e, r, t: (e, r, 1 - t)
    shift = lambda s: lambda e, r, t: ((e + s) % n_e, r, t)

    def add(a, b):
        return (a.astype(jnp.float32) + b.astype(jnp.float32)).astype(jnp.bfloat16)

    def after(x, *deps):
        return lax.optimization_barrier((x, *deps))[0]

    first_core = t == 0

    named = routes[:, :, None] == jnp.arange(n_exp, dtype=jnp.int32)[None, None, :]
    dense = jnp.sum(jnp.where(named, gates[:, :, None], 0.0), axis=1)
    coarse = lax.reduce_precision(dense, 8, 7)
    beside = jnp.concatenate([coarse, dense - coarse], axis=1).astype(jnp.bfloat16)
    beside = jnp.pad(beside, ((0, 0), (0, -2 * n_exp % 128)))
    mine = jnp.where(first_core, tokens, cotangent)
    mine = jnp.concatenate([mine, beside], axis=1)
    expert = (e * exp_local + r).astype(jnp.int32)
    ids = jnp.stack([t.astype(jnp.int32), expert, r.astype(jnp.int32)])
    w_in, w_down = weights(ids, gate_weight, up_weight, down_weight)

    n = n_e
    last = n - 1
    plane, two, sent_b, mine_of, other_of, done = ([None] * n for _ in range(6))
    summed, half_way, most = ([None] * n for _ in range(3))

    def grad(chunks, at, had, *deps):
        swap = at == 4
        total = None
        for begin in range(0, len(chunks), 4):
            group = chunks[begin : begin + 4]
            part = weight_grad(
                after(ids, *deps),
                width,
                [mine_of[j] for j in group],
                [other_of[j] for j in group],
                [done[j][at] for j in group],
                had,
                swap,
                jnp.bfloat16 if len(chunks) <= 4 else jnp.float32,
            )
            total = part if total is None else total + part
        return total.astype(jnp.bfloat16)

    early, late = range(2), range(n - 2, n)
    if n > 4:
        early = range(n - 2)

    plane[0] = mine
    plane[1] = send(mine, shift(-1))
    two[0] = after(jnp.concatenate([mine, send(mine, plane_a)]), w_in, w_down)
    sent_b[0] = send(two[0], plane_b)
    came_lo = send(two[0], core)
    came_a = send(plane[1], plane_a)
    plane[2] = send(plane[1], shift(-1))
    two[1] = after(jnp.concatenate([plane[1], came_a]), plane[2], came_lo)

    home = {}
    for i in range(1, n + 1):
        beside = {}
        if i < n:
            sent_b[i] = send(two[i], plane_b)
        if i + 1 < n:
            beside["a"] = send(plane[i + 1], plane_a)
        if i + 2 < n:
            beside["z"] = send(plane[i + 1], shift(-1))
        if i >= 2:
            came_core = send(done[i - 2][1], core)
            summed[i - 2] = add(done[i - 2][0], came_core)
        if i == 3:
            beside["far"] = send(summed[1][2 * rows :], shift(1))
        if i == 4:
            beside["own"] = send(far, plane_b)
            beside["near"] = send(summed[1][: 2 * rows], shift(1))
        if i >= 4:
            beside["b"] = send(summed[i - 2][2 * rows :], plane_b)
        if i >= 5:
            beside["home"] = send(half_way[i - 3][rows:], plane_a)
        if i >= 6:
            home[i - 4] = send(most[i - 4], shift(i - 4))
        arrived = sent_b[i - 1]
        if i < n:
            arrived = after(arrived, two[i], *([summed[i - 2]] if i >= 2 else []))
        mine_of[i - 1] = (two[i - 1], arrived)
        came_hi = send(arrived, core)
        if i >= 2:
            came_hi, summed[i - 2] = lax.optimization_barrier((came_hi, summed[i - 2]))
        if i < n:
            beside["lo"] = send(two[i], core)
        other_of[i - 1] = (came_lo, came_hi)
        done[i - 1] = chunk(ids, mine_of[i - 1], other_of[i - 1], n_exp, w_in, w_down)
        if i == early[-1] + 1:
            beside["grads"] = [grad(early, at, (), done[i - 1][0]) for at in (2, 3, 4)]
        beside, done[i - 1] = lax.optimization_barrier((beside, done[i - 1]))
        if i < n:
            sent_b[i] = after(sent_b[i], done[i - 1][0])
        if i == early[-1] + 1:
            gate_had, up_had, down_had = beside["grads"]
        came_lo = beside.get("lo")
        if i + 1 < n:
            two[i + 1] = jnp.concatenate([plane[i + 1], beside["a"]])
        if i + 2 < n:
            plane[i + 2] = beside["z"]
        if i == 3:
            far = add(summed[0][2 * rows :], beside["far"])
        if i == 4:
            near = add(summed[0][: 2 * rows], beside["near"])
            came_b = beside["own"]
        if i >= 4:
            half_way[i - 2] = add(summed[i - 2][: 2 * rows], beside["b"])
        if i >= 5:
            most[i - 3] = add(half_way[i - 3][:rows], beside["home"])

    came_core = send(done[last][1], core)
    came_home = send(half_way[n - 2][rows:], plane_a)
    if n > 4:
        home[n - 3] = send(most[n - 3], shift(n - 3))
    down_out = grad(late, 4, (down_had,), half_way[n - 2])
    came_core, came_home, home, down_out = lax.optimization_barrier(
        (came_core, came_home, home, down_out)
    )
    most[n - 2] = add(half_way[n - 2][:rows], came_home)
    summed[last] = add(done[last][0], came_core)

    home[n - 2] = send(most[n - 2], shift(n - 2))
    to_b = send(summed[last][2 * rows :], plane_b)
    gate_out = grad(late, 2, (gate_had,), summed[last])
    to_b, gate_out = lax.optimization_barrier((to_b, gate_out))
    half_way[last] = add(summed[last][: 2 * rows], to_b)

    came_home = send(half_way[last][rows:], plane_a)
    came_home, home = lax.optimization_barrier((came_home, home))
    most[last] = add(half_way[last][:rows], came_home)

    home[last] = send(most[last], shift(last))
    near = add(near, came_b)
    own = after(near[rows:], half_way[last])
    own = send(own, plane_a).astype(jnp.float32)
    up_out = grad(late, 3, (up_had,), most[last])
    most[0] = own + near[:rows].astype(jnp.float32)

    total = most[0].astype(jnp.float32)
    for s in range(2, n):
        total = total + home[s].astype(jnp.float32)
    return total.astype(jnp.bfloat16), gate_out, up_out, down_out


def solution(mesh):
    in_specs = (
        P(("expert", "replica"), None),
        P(("expert", "replica"), None),
        P(("expert", "replica"), None),
        P(("expert", "replica"), None),
        P("expert", None, "tensor"),
        P("expert", None, "tensor"),
        P("expert", "tensor", None),
    )
    out_specs = (
        P(("expert", "replica"), "tensor"),
        P(("expert", "replica"), None, "tensor"),
        P(("expert", "replica"), None, "tensor"),
        P(("expert", "replica"), "tensor", None),
    )
    return jax.shard_map(body, mesh=mesh, in_specs=in_specs, out_specs=out_specs, check_vma=False)
```

```python
import functools

import jax
import jax.numpy as jnp
from jax import lax
from jax.experimental import pallas as pl
from jax.experimental.pallas import tpu as pltpu
from jax.sharding import PartitionSpec as P

AXES = ("expert", "replica", "tensor")
PICK_LIMIT = 58 * 1024 * 1024
CHUNK_LIMIT = 26 * 1024 * 1024
WEIGHT_LIMIT = 26 * 1024 * 1024
ARRIVAL = ((0, 1, 2, 3), (0, 2, 1, 3))
LAST = (((1,), (1,)), ((), ()))


def permutation(sizes, target):
    n_e, n_r, n_t = sizes
    pairs = []
    for e in range(n_e):
        for r in range(n_r):
            for t in range(n_t):
                te, tr, tt = target(e, r, t)
                pairs.append(((e * n_r + r) * n_t + t, (te * n_r + tr) * n_t + tt))
    return pairs


def pick_kernel(ids, gate, up, down, w_in, w_down, sem):
    half = gate.shape[2]
    copies = [
        pltpu.make_async_copy(gate.at[ids[2]], w_in.at[:, pl.ds(0, half)], sem.at[0]),
        pltpu.make_async_copy(up.at[ids[2]], w_in.at[:, pl.ds(half, half)], sem.at[1]),
        pltpu.make_async_copy(down.at[ids[2]], w_down, sem.at[2]),
    ]
    for copy in copies:
        copy.start()
    for copy in copies:
        copy.wait()


def weights(ids, gate, up, down):
    _, width, half = gate.shape
    vmem = pl.BlockSpec(memory_space=pltpu.VMEM)
    return pl.pallas_call(
        pick_kernel,
        out_shape=(
            jax.ShapeDtypeStruct((width, 2 * half), jnp.bfloat16),
            jax.ShapeDtypeStruct((half, width), jnp.bfloat16),
        ),
        in_specs=[pl.BlockSpec(memory_space=pltpu.SMEM)]
        + [pl.BlockSpec(memory_space=pl.ANY)] * 3,
        out_specs=(vmem, vmem),
        scratch_shapes=[pltpu.SemaphoreType.DMA((3,))],
        compiler_params=pltpu.CompilerParams(vmem_limit_bytes=PICK_LIMIT),
        name="pick",
    )(ids, gate, up, down)


def chunk_kernel(n_exp, ids, mine_lo, mine_hi, other_lo, other_hi, w_in, w_down, *refs):
    keep, going, gate_t, up_t, hidden_t, pre, back = refs
    rows = mine_lo.shape[0] // 2
    half = w_down.shape[0]
    width = w_in.shape[0]
    half_width = width // 2
    lanes = mine_lo.shape[1] - width
    lane = lax.broadcasted_iota(jnp.int32, (rows, lanes), 1)
    mask = (lane == ids[1]) | (lane == ids[1] + n_exp)

    def run(t):
        mine, other = (mine_lo, mine_hi), (other_lo, other_hi)
        xs, cs = (mine, other) if t == 0 else (other, mine)
        for h in range(2):
            both = pl.ds(2 * h * rows, 2 * rows)
            pre[both, :] = jnp.dot(
                xs[h][:, :width], w_in[...], preferred_element_type=jnp.float32
            )
            back[both, :] = lax.dot_general(
                cs[h][:, :width], w_down[...], LAST, preferred_element_type=jnp.float32
            )
        pieces = []
        for i in range(4):
            at = ARRIVAL[1].index(i)
            here, there = pl.ds(i * rows, rows), pl.ds(at * rows, rows)
            g = xs[i // 2][pl.ds(i % 2 * rows, rows), width:].astype(jnp.float32)
            g = jnp.sum(jnp.where(mask, g, 0.0), axis=1, keepdims=True)
            gate_pre, up_proj = pre[here, :half], pre[here, half:]
            hidden_grad = g * back[there, :]
            sig = 1.0 / (1.0 + jnp.exp(-gate_pre))
            act = gate_pre * sig
            up_grad = hidden_grad * act
            gate_grad = hidden_grad * up_proj * sig * (1.0 + gate_pre * (1.0 - sig))
            hidden = g * (act * up_proj)
            gate_t[:, here] = gate_grad.T.astype(jnp.bfloat16)
            up_t[:, here] = up_grad.T.astype(jnp.bfloat16)
            hidden_t[:, there] = hidden.T.astype(jnp.bfloat16)
            pieces.append(
                jnp.concatenate(
                    [gate_grad.astype(jnp.bfloat16), up_grad.astype(jnp.bfloat16)], axis=1
                )
            )
        grads = jnp.concatenate(pieces, axis=0)
        for h in range(2):
            part = lax.dot_general(
                grads,
                w_in[h * half_width : (h + 1) * half_width, :],
                LAST,
                preferred_element_type=jnp.float32,
            ).astype(jnp.bfloat16)
            out = keep if h == t else going
            for i in range(4):
                at = ARRIVAL[h].index(i)
                out[at * rows : (at + 1) * rows, :] = part[i * rows : (i + 1) * rows, :]

    @pl.when(ids[0] == 0)
    def _():
        run(0)

    @pl.when(ids[0] == 1)
    def _():
        run(1)


def chunk(ids, mine, other, n_exp, w_in, w_down):
    n, width = 2 * mine[0].shape[0], w_in.shape[0]
    half = w_down.shape[0]
    vmem = pl.BlockSpec(memory_space=pltpu.VMEM)
    bf16 = jnp.bfloat16
    return pl.pallas_call(
        functools.partial(chunk_kernel, n_exp),
        out_shape=(
            jax.ShapeDtypeStruct((n, width // 2), bf16),
            jax.ShapeDtypeStruct((n, width // 2), bf16),
            jax.ShapeDtypeStruct((half, n), bf16),
            jax.ShapeDtypeStruct((half, n), bf16),
            jax.ShapeDtypeStruct((half, n), bf16),
        ),
        in_specs=[pl.BlockSpec(memory_space=pltpu.SMEM)]
        + [vmem] * 6,
        out_specs=(vmem,) * 5,
        scratch_shapes=[
            pltpu.VMEM((n, 2 * half), jnp.float32),
            pltpu.VMEM((n, half), jnp.float32),
        ],
        compiler_params=pltpu.CompilerParams(vmem_limit_bytes=CHUNK_LIMIT),
        cost_estimate=pl.CostEstimate(flops=1, bytes_accessed=1, transcendentals=0),
        name="chunk",
    )(ids, *mine, *other, w_in, w_down)


def weight_kernel(k, swap, carried, ids, *refs):
    mine, other, left = refs[: 2 * k], refs[2 * k : 4 * k], refs[4 * k : 5 * k]
    refs = refs[5 * k :]
    if carried:
        had, refs = refs[0], refs[1:]
    out, buf, sem = refs
    n = buf.shape[1] // 2

    def fetch(j, start):
        for t in range(2):

            @pl.when(ids[0] == t)
            def _():
                src = mine if (t == 1) == swap else other
                for h in range(2):
                    copy = pltpu.make_async_copy(
                        src[2 * j + h].at[:, pl.ds(0, buf.shape[2])],
                        buf.at[j, pl.ds(h * n, n)],
                        sem.at[j, h],
                    )
                    copy.start() if start else copy.wait()

    for j in range(k):
        fetch(j, True)
    total = None
    for j in range(k):
        fetch(j, False)
        part = jnp.dot(left[j][...], buf[j], preferred_element_type=jnp.float32)
        total = part if total is None else total + part
    total = total if swap else total.T
    if carried:
        total = total + had[0].astype(jnp.float32)
    out[0] = total.astype(out.dtype)


def weight_grad(ids, width, mine, other, left, had, swap, dtype):
    k, n, half = len(left), 2 * mine[0][0].shape[0], left[0].shape[0]
    vmem = pl.BlockSpec(memory_space=pltpu.VMEM)
    return pl.pallas_call(
        functools.partial(weight_kernel, k, swap, len(had)),
        out_shape=jax.ShapeDtypeStruct((1, half, width) if swap else (1, width, half), dtype),
        in_specs=[pl.BlockSpec(memory_space=pltpu.SMEM)]
        + [pl.BlockSpec(memory_space=pl.ANY)] * (4 * k)
        + [vmem] * (k + len(had)),
        out_specs=vmem,
        scratch_shapes=[
            pltpu.VMEM((k, n, width), jnp.bfloat16),
            pltpu.SemaphoreType.DMA((k, 2)),
        ],
        compiler_params=pltpu.CompilerParams(vmem_limit_bytes=WEIGHT_LIMIT),
        name="weight_grad",
    )(ids, *[h for m in mine for h in m], *[h for o in other for h in o], *left, *had)


def body(tokens, cotangent, routes, gates, gate_weight, up_weight, down_weight):
    rows, width = tokens.shape
    exp_local = gate_weight.shape[0]
    sizes = tuple(lax.axis_size(a) for a in AXES)
    n_e, n_r, n_t = sizes
    assert n_e >= 4 and n_r == 4 and n_t == 2 and exp_local == n_r
    e, r, t = (lax.axis_index(a) for a in AXES)
    n_exp = exp_local * n_e

    def send(x, target):
        return lax.ppermute(x, AXES, permutation(sizes, target))

    plane_a = lambda e, r, t: (e, r ^ (1 + t), t)
    plane_b = lambda e, r, t: (e, r ^ (2 - t), t)
    core = lambda e, r, t: (e, r, 1 - t)
    shift = lambda s: lambda e, r, t: ((e + s) % n_e, r, t)

    def add(a, b):
        return (a.astype(jnp.float32) + b.astype(jnp.float32)).astype(jnp.bfloat16)

    def after(x, *deps):
        return lax.optimization_barrier((x, *deps))[0]

    first_core = t == 0

    named = routes[:, :, None] == jnp.arange(n_exp, dtype=jnp.int32)[None, None, :]
    dense = jnp.sum(jnp.where(named, gates[:, :, None], 0.0), axis=1)
    coarse = lax.reduce_precision(dense, 8, 7)
    beside = jnp.concatenate([coarse, dense - coarse], axis=1).astype(jnp.bfloat16)
    beside = jnp.pad(beside, ((0, 0), (0, -2 * n_exp % 128)))
    mine = jnp.where(first_core, tokens, cotangent)
    mine = jnp.concatenate([mine, beside], axis=1)
    expert = (e * exp_local + r).astype(jnp.int32)
    ids = jnp.stack([t.astype(jnp.int32), expert, r.astype(jnp.int32)])
    w_in, w_down = weights(ids, gate_weight, up_weight, down_weight)

    n = n_e
    last = n - 1
    plane, two, sent_b, mine_of, other_of, done = ([None] * n for _ in range(6))
    summed, half_way, most = ([None] * n for _ in range(3))

    def grad(chunks, at, had, *deps):
        swap = at == 4
        total = None
        for begin in range(0, len(chunks), 4):
            group = chunks[begin : begin + 4]
            part = weight_grad(
                after(ids, *deps),
                width,
                [mine_of[j] for j in group],
                [other_of[j] for j in group],
                [done[j][at] for j in group],
                had,
                swap,
                jnp.bfloat16 if len(chunks) <= 4 else jnp.float32,
            )
            total = part if total is None else total + part
        return total.astype(jnp.bfloat16)

    early, late = range(2), range(n - 2, n)
    if n > 4:
        early = range(n - 2)

    plane[0] = mine
    plane[1] = send(mine, shift(-1))
    two[0] = after(jnp.concatenate([mine, send(mine, plane_a)]), w_in, w_down)
    sent_b[0] = send(two[0], plane_b)
    came_lo = send(two[0], core)
    came_a = send(plane[1], plane_a)
    plane[2] = send(plane[1], shift(-1))
    two[1] = after(jnp.concatenate([plane[1], came_a]), plane[2], came_lo)

    home = {}
    for i in range(1, n + 1):
        beside = {}
        if i < n:
            sent_b[i] = send(two[i], plane_b)
        if i + 1 < n:
            beside["a"] = send(plane[i + 1], plane_a)
        if i + 2 < n:
            beside["z"] = send(plane[i + 1], shift(-1))
        if i >= 2:
            came_core = send(done[i - 2][1], core)
            summed[i - 2] = add(done[i - 2][0], came_core)
        if i == 3:
            beside["far"] = send(summed[1][2 * rows :], shift(1))
        if i == 4:
            beside["own"] = send(far, plane_b)
            beside["near"] = send(summed[1][: 2 * rows], shift(1))
        if i >= 4:
            beside["b"] = send(summed[i - 2][2 * rows :], plane_b)
        if i >= 5:
            beside["home"] = send(half_way[i - 3][rows:], plane_a)
        if i >= 6:
            home[i - 4] = send(most[i - 4], shift(i - 4))
        arrived = sent_b[i - 1]
        if i < n:
            arrived = after(arrived, two[i], *([summed[i - 2]] if i >= 2 else []))
        mine_of[i - 1] = (two[i - 1], arrived)
        came_hi = send(arrived, core)
        if i >= 2:
            came_hi, summed[i - 2] = lax.optimization_barrier((came_hi, summed[i - 2]))
        if i < n:
            beside["lo"] = send(two[i], core)
        other_of[i - 1] = (came_lo, came_hi)
        done[i - 1] = chunk(ids, mine_of[i - 1], other_of[i - 1], n_exp, w_in, w_down)
        if i == early[-1] + 1:
            beside["grads"] = [grad(early, at, (), done[i - 1][0]) for at in (2, 3, 4)]
        beside, done[i - 1] = lax.optimization_barrier((beside, done[i - 1]))
        if i < n:
            sent_b[i] = after(sent_b[i], done[i - 1][0])
        if i == early[-1] + 1:
            gate_had, up_had, down_had = beside["grads"]
        came_lo = beside.get("lo")
        if i + 1 < n:
            two[i + 1] = jnp.concatenate([plane[i + 1], beside["a"]])
        if i + 2 < n:
            plane[i + 2] = beside["z"]
        if i == 3:
            far = add(summed[0][2 * rows :], beside["far"])
        if i == 4:
            near = add(summed[0][: 2 * rows], beside["near"])
            came_b = beside["own"]
        if i >= 4:
            half_way[i - 2] = add(summed[i - 2][: 2 * rows], beside["b"])
        if i >= 5:
            most[i - 3] = add(half_way[i - 3][:rows], beside["home"])

    came_core = send(done[last][1], core)
    came_home = send(half_way[n - 2][rows:], plane_a)
    if n > 4:
        home[n - 3] = send(most[n - 3], shift(n - 3))
    came_core, came_home, home = lax.optimization_barrier((came_core, came_home, home))
    most[n - 2] = add(half_way[n - 2][:rows], came_home)
    summed[last] = add(done[last][0], came_core)

    home[n - 2] = send(most[n - 2], shift(n - 2))
    to_b = send(summed[last][2 * rows :], plane_b)
    gate_out = grad(late, 2, (gate_had,), summed[last])
    to_b, gate_out = lax.optimization_barrier((to_b, gate_out))
    half_way[last] = add(summed[last][: 2 * rows], to_b)

    came_home = send(half_way[last][rows:], plane_a)
    down_out = grad(late, 4, (down_had,), half_way[last])
    came_home, home, down_out = lax.optimization_barrier((came_home, home, down_out))
    most[last] = add(half_way[last][:rows], came_home)

    home[last] = send(most[last], shift(last))
    near = add(near, came_b)
    own = after(near[rows:], half_way[last])
    own = send(own, plane_a).astype(jnp.float32)
    up_out = grad(late, 3, (up_had,), most[last])
    most[0] = own + near[:rows].astype(jnp.float32)

    total = most[0].astype(jnp.float32)
    for s in range(2, n):
        total = total + home[s].astype(jnp.float32)
    return total.astype(jnp.bfloat16), gate_out, up_out, down_out


def solution(mesh):
    in_specs = (
        P(("expert", "replica"), None),
        P(("expert", "replica"), None),
        P(("expert", "replica"), None),
        P(("expert", "replica"), None),
        P("expert", None, "tensor"),
        P("expert", None, "tensor"),
        P("expert", "tensor", None),
    )
    out_specs = (
        P(("expert", "replica"), "tensor"),
        P(("expert", "replica"), None, "tensor"),
        P(("expert", "replica"), None, "tensor"),
        P(("expert", "replica"), "tensor", None),
    )
    return jax.shard_map(body, mesh=mesh, in_specs=in_specs, out_specs=out_specs, check_vma=False)
```
